32 devices in a mesh: pairs: 8 (over z, y), coup: 4 (over x, core).
Axes of the slice: x: 2, y: 2, z: 4, core: 2. Of those that a mesh axis runs over, the one named last changes fastest.
Arguments:
- coupling_list: int32 [3, 128], P(None, 'pairs'), may hold values from 0 to 127, as said below
- pair_slot: int32 [32], replicated, may hold values from 0 to 31, as said below
- coupling_weight: float32 [128], P('pairs'), may hold values from -1 to 1
- integrals: bfloat16 [32, 448, 448], P(('pairs', 'coup')), may hold values from -6 to 6
- orbital_energy: float32 [32, 448], P(('pairs', 'coup')), may hold values from 0.5 to 3
- pair_energy: float32 [32], P(('pairs', 'coup')), may hold values from 0.3 to 3
- intersections: bfloat16 [128, 448, 448], P(('pairs', 'coup')), may hold values from -0.25 to 0.25
Outputs:
- amplitudes: float32 [32, 448, 448], P(('pairs', 'coup'))
The draws below stay inside these ranges and needn't reach their ends.
Inputs may be any that keep to these rules, and one draw needn't show every extreme that they name: `coupling_list`: row 0 and row 1 hold pair numbers, row 2 an intersection index. Positions g * 16 to (g + 1) * 16 - 1 form block g: its pairs i have rows (pair_slot) in g * 4 to (g + 1) * 4 - 1 and its intersection indices lie in g * 16 to (g + 1) * 16 - 1; for every h, exactly two couplings of block g have pair j with its row in h * 4 to (h + 1) * 4 - 1, and both name the same pair j. In each block at most 8 couplings have pair i with its row in the same 1 row of one device, and exactly 8 do for one such device. Likewise in each block at most 8 couplings have an intersection index among the same 4 indices of one device, and exactly 8 do for one such device. `pair_slot`: A permutation of the pairs.
All inputs are finite; a program needn't handle non-finite values.
Results may differ from the reference program's by a relative error of at most 0.0024.
Values may be sent and summed in bfloat16 or wider, within the bound.
A program may use at most 128 MiB of HBM per device.

```python
import math
from functools import partial
import jax
import jax.numpy as jnp
from jax import lax

NV = 448
PAIR_DEV = 1
OV_DEV = 4
ITERS = 2
TOTAL_PAIRS = 32
GROUP_PAIRS = 4
TOTAL_INTERSECTIONS = 128
GROUP_INTERSECTIONS = 16
GROUP_COUPLINGS = 16
TOTAL_COUPLINGS = 128
HCAP = 8
N_PAIRS = 8
N_COUP = 4


def slot_table(key):
    return jax.random.permutation(jax.random.fold_in(key, 11), TOTAL_PAIRS).astype(jnp.int32)


def draw_pair_slot(key, part):
    return slot_table(key)


def capped_members(key, rank_salt, busy_salt):
    shuffler = jax.vmap(partial(jax.random.permutation, x=GROUP_COUPLINGS))
    load_rank = shuffler(jax.random.split(jax.random.fold_in(key, rank_salt), N_PAIRS)).astype(jnp.int32)
    busiest = jax.random.randint(jax.random.fold_in(key, busy_salt), (N_PAIRS, 1), 0, N_COUP)
    spare = (busiest + 1 + (load_rank - HCAP) % (N_COUP - 1)) % N_COUP
    return jnp.where(load_rank < HCAP, busiest, spare)


def draw_coupling_list(key, part):
    slot_of_pair = slot_table(key)
    pair_of_row = jnp.argsort(slot_of_pair).astype(jnp.int32)
    group_ids = jnp.arange(N_PAIRS, dtype=jnp.int32)[:, None]
    shuffler = jax.vmap(partial(jax.random.permutation, x=GROUP_COUPLINGS))
    read_rank = shuffler(jax.random.split(jax.random.fold_in(key, 21), N_PAIRS)).astype(jnp.int32)
    source_group = read_rank // 2
    read_pick = jax.random.randint(jax.random.fold_in(key, 22), (N_PAIRS, N_PAIRS), 0, GROUP_PAIRS)
    read_row = source_group * GROUP_PAIRS + jnp.take_along_axis(read_pick, source_group, axis=1)
    owner_member = capped_members(key, 23, 24)
    within = jax.random.randint(jax.random.fold_in(key, 25), (N_PAIRS, GROUP_COUPLINGS), 0, PAIR_DEV)
    owner_row = group_ids * GROUP_PAIRS + owner_member * PAIR_DEV + within
    intersection_member = capped_members(key, 27, 28)
    intersection_within = jax.random.randint(jax.random.fold_in(key, 26), (N_PAIRS, GROUP_COUPLINGS), 0, OV_DEV)
    intersection_index = group_ids * GROUP_INTERSECTIONS + intersection_member * OV_DEV + intersection_within
    pair_first = pair_of_row[owner_row.reshape(-1)]
    pair_second = pair_of_row[read_row.reshape(-1)]
    return jnp.stack([pair_first, pair_second, intersection_index.reshape(-1)]).astype(jnp.int32)


def block_levels(rng, shape, cuts, least, high):
    def one(axis_at, shards_of):
        draws = jax.random.uniform(jax.random.fold_in(jax.random.fold_in(rng, 6), axis_at), (shards_of,), jnp.float32, least / len(cuts), high / len(cuts))
        return jnp.repeat(jnp.exp(draws), shape[axis_at] // shards_of).reshape((-1,) + (1,) * (len(shape) - axis_at - 1))

    gain = one(*cuts[0])
    for cut in cuts[1:]:
        gain = gain * one(*cut)
    return gain


def centred(stream_key, extent, width, bound, pieces=(), held_as=jnp.bfloat16):
    result = jax.random.normal(stream_key, extent, jnp.float32) * width
    if len(pieces) > 0:
        result = block_levels(stream_key, extent, pieces, -0.22, 0.18) * result
    return jnp.clip(result, min=-bound, max=bound).astype(held_as)


def setup_inputs(seed: int = 0) -> dict:
    arg_keys = jax.random.split(jax.random.key(seed), 8)
    return {
        "coupling_list": draw_coupling_list(jax.random.fold_in(arg_keys[7], 71), 0),
        "pair_slot": draw_pair_slot(jax.random.fold_in(arg_keys[7], 71), 0),
        "coupling_weight": jnp.clip(jax.random.uniform(arg_keys[2], (TOTAL_COUPLINGS,), jnp.float32, -1.0, 1.0) * block_levels(arg_keys[2], (TOTAL_COUPLINGS,), ((0, 8),), -0.4, 0.0), -1.0, 1.0),
        "integrals": centred(arg_keys[3], (TOTAL_PAIRS, NV, NV), 1.0, 6.0, ((0, 32),)),
        "orbital_energy": jnp.clip(0.5 + 2.5 * jax.random.uniform(arg_keys[4], (TOTAL_PAIRS, NV), jnp.float32) ** block_levels(arg_keys[4], (TOTAL_PAIRS, NV), ((0, 32),), -0.2, 0.2), 0.5, 3.0),
        "pair_energy": jnp.clip(jnp.exp(math.log(3.0) - 2.3025851 * jax.random.uniform(arg_keys[5], (TOTAL_PAIRS,), jnp.float32) ** block_levels(arg_keys[5], (TOTAL_PAIRS,), ((0, 32),), -0.2, 0.2)), 0.3, 3.0),
        "intersections": centred(arg_keys[6], (TOTAL_INTERSECTIONS, NV, NV), NV ** -0.5, 0.25, ((0, 32),)),
    }


def reference(coupling_list, pair_slot, coupling_weight, integrals, orbital_energy, pair_energy, intersections):
    owner_row = pair_slot[coupling_list[0]].astype(jnp.int32)
    reader_row = pair_slot[coupling_list[1]].astype(jnp.int32)
    intersection_index = coupling_list[2].astype(jnp.int32)
    denominator = orbital_energy[:, :, None] + orbital_energy[:, None, :] + pair_energy[:, None, None]
    integral_f = integrals.astype(jnp.float32)
    amplitudes = -integral_f / denominator
    total = coupling_list.shape[1]
    block_size = math.gcd(total, 64)
    for iteration in range(ITERS):
        rounded = amplitudes.astype(jnp.bfloat16)

        def accumulate(block_turn, coupled):
            first_slot = (block_turn * block_size).astype(jnp.int32)
            read_block = lax.dynamic_slice_in_dim(reader_row, first_slot, block_size)
            owner_block = lax.dynamic_slice_in_dim(owner_row, first_slot, block_size)
            intersection_block = lax.dynamic_slice_in_dim(intersection_index, first_slot, block_size)
            weight_block = lax.dynamic_slice_in_dim(coupling_weight, first_slot, block_size)
            amp_block = rounded[read_block].astype(jnp.float32)
            ovl_block = intersections[intersection_block].astype(jnp.float32)
            left_product = jnp.einsum("sab,sbc->sac", ovl_block, amp_block).astype(jnp.bfloat16)
            left_product = lax.optimization_barrier(left_product).astype(jnp.float32)
            full_product = jnp.einsum("sac,sdc->sad", left_product, ovl_block)
            return coupled.at[owner_block].add(weight_block[:, None, None] * full_product)

        coupled = lax.fori_loop(0, total // block_size, accumulate, jnp.zeros(amplitudes.shape, jnp.float32))
        amplitudes = -(integral_f + coupled) / denominator
    return amplitudes
```

```python
import functools

import jax
import jax.numpy as jnp
from jax import lax
from jax.experimental import pallas as pl
from jax.experimental.pallas import tpu as pltpu
from jax.sharding import PartitionSpec as P

ITERS = 2
MESH = pl.DeviceIdType.MESH
VMEM_LIMIT = 48 * 1024 * 1024


def lookup(lookup_table, queries):
    columns = lax.broadcasted_iota(jnp.int32, (queries.shape[0], lookup_table.shape[0]), 1)
    return jnp.sum(jnp.where(queries[:, None] == columns, lookup_table[None, :], 0), axis=1)


def remote(src, dst, send_sem, recv_sem, device_id):
    copy = pltpu.make_async_remote_copy(
        src_ref=src, dst_ref=dst, send_sem=send_sem, recv_sem=recv_sem,
        device_id=device_id, device_id_type=MESH,
    )
    copy.start()
    return copy


def send_strips(amp_ref, strips, send_sem, recv_sem, m, coup_total):
    rows = strips.shape[2]
    copies = []
    for d in range(1, coup_total):
        q = lax.rem(m + d, coup_total)
        copies.append(remote(
            amp_ref.at[:, pl.ds(pl.multiple_of(q * rows, 16), rows), :],
            strips.at[m], send_sem.at[d], recv_sem.at[d], {"coup": q},
        ))
    strips[m] = amp_ref[:, pl.ds(pl.multiple_of(m * rows, 16), rows), :]
    return copies


def send_picks(wanted, strips, outbuf, arrived, send_sem, recv_sem, g, group_total):
    pair_dev = strips.shape[1]
    copies = []
    for d in list(range(1, group_total)) + [0]:
        h = lax.rem(g + d, group_total)
        pick = wanted[h, 0, 0]
        if pair_dev == 1:
            block = strips[pick, 0]
        else:
            block = strips[pick // pair_dev, pick % pair_dev]
        if d == 0:
            arrived[g] = block
        else:
            outbuf[d] = block
            copies.append(remote(
                outbuf.at[d], arrived.at[g], send_sem.at[d], recv_sem.at[d], {"pairs": h}
            ))
    return copies


def greet(coords_list):
    barrier = pltpu.get_barrier_semaphore()
    for coords in coords_list:
        pl.semaphore_signal(barrier, inc=1, device_id=coords, device_id_type=MESH)
    pl.semaphore_wait(barrier, len(coords_list))


def first_exchange(
    group_total, coup_total, amp_ref, ask_ref, x_ref, arrived, x_all, asked, strips, outbuf, wanted,
    strip_send, strip_recv, ask_send, ask_recv, pick_send, pick_recv,
    far_send, far_recv, sib_send, sib_recv, fwd_send, fwd_recv, local_sem, want_sem,
):
    g, m = lax.axis_index("pairs"), lax.axis_index("coup")
    ov_dev = x_ref.shape[0]
    chips = coup_total // 2
    chip, core = m // 2, lax.rem(m, 2)
    sibling = chip * 2 + 1 - core
    greet(
        [{"coup": lax.rem(m + d, coup_total)} for d in range(1, coup_total)]
        + [{"pairs": lax.rem(g + d, group_total)} for d in range(1, group_total)]
    )
    strip_copies = send_strips(amp_ref, strips, strip_send, strip_recv, m, coup_total)
    ask_copies = []
    for d in range(1, group_total):
        h = lax.rem(g + d, group_total)
        ask_copies.append(remote(
            ask_ref.at[h], asked.at[g], ask_send.at[d], ask_recv.at[d], {"pairs": h}
        ))
    asked[g] = ask_ref[g]
    far_copies = []
    for i in range(ov_dev):
        for d in range(1, chips):
            peer = lax.rem(chip + d, chips) * 2 + core
            far_copies.append((d, i, remote(
                x_ref.at[i], x_all.at[m * ov_dev + i],
                far_send.at[d, i], far_recv.at[d, i], {"coup": peer},
            )))
    sib_copy = remote(
        x_ref, x_all.at[pl.ds(m * ov_dev, ov_dev)], sib_send, sib_recv, {"coup": sibling}
    )
    own_copy = pltpu.make_async_copy(x_ref, x_all.at[pl.ds(m * ov_dev, ov_dev)], local_sem)
    own_copy.start()
    for copy in ask_copies:
        copy.wait_recv()
    want_copy = pltpu.make_async_copy(asked, wanted, want_sem)
    want_copy.start()
    want_copy.wait()
    for copy in strip_copies:
        copy.wait_recv()
    pick_copies = send_picks(
        wanted, strips, outbuf, arrived, pick_send, pick_recv, g, group_total
    )
    forwards = []
    for d, i, copy in far_copies:
        copy.wait_recv()
        origin = lax.rem(chip - d + chips, chips) * 2 + core
        slot = x_all.at[origin * ov_dev + i]
        forwards.append(remote(
            slot, slot, fwd_send.at[d, i], fwd_recv.at[d, i], {"coup": sibling}
        ))
    own_copy.wait()
    sib_copy.wait()
    for copy in forwards + pick_copies:
        copy.wait()
    for copy in strip_copies + ask_copies + [c for _, _, c in far_copies]:
        copy.wait_send()


def later_exchange(
    group_total, coup_total, amp_ref, wanted, arrived, strips, outbuf,
    strip_send, strip_recv, pick_send, pick_recv,
):
    g, m = lax.axis_index("pairs"), lax.axis_index("coup")
    greet(
        [{"coup": lax.rem(m + d, coup_total)} for d in range(1, coup_total)]
        + [{"pairs": lax.rem(g + d, group_total)} for d in range(1, group_total)]
    )
    strip_copies = send_strips(amp_ref, strips, strip_send, strip_recv, m, coup_total)
    for copy in strip_copies:
        copy.wait_recv()
    pick_copies = send_picks(
        wanted, strips, outbuf, arrived, pick_send, pick_recv, g, group_total
    )
    for copy in pick_copies:
        copy.wait()
    for copy in strip_copies:
        copy.wait_send()


def reduce_partials(
    coup_total, part, total, near, joined, far, near_send, near_recv, far_send, far_recv
):
    m = lax.axis_index("coup")
    chips = coup_total // 2
    chip, core = m // 2, lax.rem(m, 2)
    sibling = chip * 2 + 1 - core
    peers = [lax.rem(chip + d, chips) * 2 for d in range(chips)]
    greet([{"coup": sibling}] + [{"coup": peers[d] + core} for d in range(1, chips)])
    order = list(range(1, chips)) + [0]
    near_copies = {}
    for d in order:
        near_copies[d] = remote(
            part.at[peers[d] + 1 - core], near.at[d], near_send.at[d], near_recv.at[d],
            {"coup": sibling},
        )
    far_copies = []
    for d in order:
        near_copies[d].wait_recv()
        both = part[peers[d] + core].astype(jnp.float32) + near[d].astype(jnp.float32)
        if d == 0:
            total[...] = both
        else:
            joined[d] = both.astype(jnp.bfloat16)
            far_copies.append((d, remote(
                joined.at[d], far.at[d], far_send.at[d], far_recv.at[d],
                {"coup": peers[d] + core},
            )))
    for d, copy in far_copies:
        copy.wait()
        total[...] += far[d].astype(jnp.float32)
    for d in order:
        near_copies[d].wait_send()


def couple(x_index, source, owner, member, weight, amp_ref, x_ref, out_ref, acc, padded):
    k = pl.program_id(0)
    rows = amp_ref.shape[1]

    @pl.when(k == 0)
    def _():
        acc[...] = jnp.zeros_like(acc)
        padded[...] = jnp.zeros_like(padded)

    x = x_ref[0]
    right = lax.dot_general(
        amp_ref[source[k]], x, (((1,), (1,)), ((), ())), preferred_element_type=jnp.float32
    )
    padded[pl.ds(pl.multiple_of(member[0] * rows, 16), rows), :] = (
        right * weight[k]
    ).astype(jnp.bfloat16)
    acc[owner[k]] += jnp.dot(x, padded[...], preferred_element_type=jnp.float32)

    @pl.when(k == pl.num_programs(0) - 1)
    def _():
        for p in range(acc.shape[0]):
            out_ref[p] = acc[p].astype(jnp.bfloat16)


def per_device(
    coupling_list, pair_slot, coupling_weight, integrals, orbital_energy, pair_energy, intersections
):
    group_total = lax.axis_size("pairs")
    coup_total = lax.axis_size("coup")
    group_index = lax.axis_index("pairs")
    member = lax.axis_index("coup")
    pair_dev, width = integrals.shape[0], integrals.shape[-1]
    ov_dev = intersections.shape[0]
    group_pairs = pair_dev * coup_total
    couplings = coupling_list.shape[1]
    rows = width // coup_total
    chips = coup_total // 2

    owner_row = lookup(pair_slot, coupling_list[0])
    reader_row = lookup(pair_slot, coupling_list[1])
    owner = owner_row - group_index * group_pairs
    source = reader_row // group_pairs
    x_index = coupling_list[2] - group_index * (ov_dev * coup_total)
    sources = lax.broadcasted_iota(jnp.int32, (group_total, couplings), 0)
    ask = jnp.max(
        jnp.where(source[None, :] == sources, (reader_row % group_pairs)[None, :], 0), axis=1
    )
    ask = jnp.broadcast_to(ask[:, None, None], (group_total, 8, 128))

    denominator = (
        orbital_energy[:, :, None] + orbital_energy[:, None, :] + pair_energy[:, None, None]
    )
    integral_f = integrals.astype(jnp.float32)
    rounded = (-integral_f / denominator).astype(jnp.bfloat16)

    vmem = pl.BlockSpec(memory_space=pltpu.VMEM)
    smem = pl.BlockSpec(memory_space=pltpu.SMEM)
    anywhere = pl.BlockSpec(memory_space=pl.ANY)
    dma = pltpu.SemaphoreType.DMA
    arrived_shape = jax.ShapeDtypeStruct((group_total, rows, width), jnp.bfloat16)
    strips_scratch = pltpu.VMEM((coup_total, pair_dev, rows, width), jnp.bfloat16)
    out_scratch = pltpu.VMEM((group_total, rows, width), jnp.bfloat16)

    def params(collective_id):
        return pltpu.CompilerParams(
            collective_id=collective_id, has_side_effects=True, vmem_limit_bytes=VMEM_LIMIT
        )

    arrived, x_all, asked = pl.pallas_call(
        functools.partial(first_exchange, group_total, coup_total),
        out_shape=(
            arrived_shape,
            jax.ShapeDtypeStruct((ov_dev * coup_total, width, width), jnp.bfloat16),
            jax.ShapeDtypeStruct((group_total, 8, 128), jnp.int32),
        ),
        in_specs=[vmem, vmem, anywhere],
        out_specs=(vmem, anywhere, vmem),
        scratch_shapes=[
            strips_scratch, out_scratch, pltpu.SMEM((group_total, 8, 128), jnp.int32),
            dma((coup_total,)), dma((coup_total,)), dma((group_total,)), dma((group_total,)),
            dma((group_total,)), dma((group_total,)),
            dma((chips, ov_dev)), dma((chips, ov_dev)), dma, dma,
            dma((chips, ov_dev)), dma((chips, ov_dev)), dma, dma,
        ],
        compiler_params=params(0),
        name="first_exchange",
    )(rounded, ask, intersections)

    for iteration in range(ITERS):
        if iteration > 0:
            arrived = pl.pallas_call(
                functools.partial(later_exchange, group_total, coup_total),
                out_shape=arrived_shape,
                in_specs=[vmem, smem],
                out_specs=vmem,
                scratch_shapes=[
                    strips_scratch, out_scratch,
                    dma((coup_total,)), dma((coup_total,)), dma((group_total,)), dma((group_total,)),
                ],
                compiler_params=params(1),
                name="later_exchange",
            )(rounded, asked)
        part = pl.pallas_call(
            couple,
            out_shape=jax.ShapeDtypeStruct((group_pairs, width, width), jnp.bfloat16),
            grid_spec=pltpu.PrefetchScalarGridSpec(
                num_scalar_prefetch=4,
                grid=(couplings,),
                in_specs=[
                    smem,
                    pl.BlockSpec((group_total, rows, width), lambda k, *_: (0, 0, 0)),
                    pl.BlockSpec((1, width, width), lambda k, xi, *_: (xi[k], 0, 0)),
                ],
                out_specs=pl.BlockSpec((group_pairs, width, width), lambda k, *_: (0, 0, 0)),
                scratch_shapes=[
                    pltpu.VMEM((group_pairs, width, width), jnp.float32),
                    pltpu.VMEM((width, width), jnp.bfloat16),
                ],
            ),
            compiler_params=pltpu.CompilerParams(vmem_limit_bytes=VMEM_LIMIT),
            name="couple",
        )(x_index, source, owner, member[None], coupling_weight, arrived, x_all)
        block = (pair_dev, width, width)
        coupled = pl.pallas_call(
            functools.partial(reduce_partials, coup_total),
            out_shape=jax.ShapeDtypeStruct(block, jnp.float32),
            in_specs=[vmem],
            out_specs=vmem,
            scratch_shapes=[
                pltpu.VMEM((chips,) + block, jnp.bfloat16),
                pltpu.VMEM((chips,) + block, jnp.bfloat16),
                pltpu.VMEM((chips,) + block, jnp.bfloat16),
                dma((chips,)), dma((chips,)), dma((chips,)), dma((chips,)),
            ],
            compiler_params=params(2),
            name="reduce_partials",
        )(part.reshape((coup_total,) + block))
        amplitudes = -(integral_f + coupled) / denominator
        rounded = amplitudes.astype(jnp.bfloat16)
    return amplitudes


def solution(mesh):
    in_specs = (
        P(None, "pairs"),
        P(),
        P("pairs"),
        P(("pairs", "coup"), None, None),
        P(("pairs", "coup"), None),
        P(("pairs", "coup")),
        P(("pairs", "coup"), None, None),
    )
    out_specs = P(("pairs", "coup"), None, None)
    return jax.shard_map(
        per_device, mesh=mesh, in_specs=in_specs, out_specs=out_specs, check_vma=False
    )
```

```python
import functools
import math

import jax
import jax.numpy as jnp
from jax import lax
from jax.experimental import pallas as pl
from jax.experimental.pallas import tpu as pltpu
from jax.sharding import PartitionSpec as P

ITERS = 2
MESH = pl.DeviceIdType.MESH
VMEM_LIMIT = 48 * 1024 * 1024


def lookup(lookup_table, queries):
    columns = lax.broadcasted_iota(jnp.int32, (queries.shape[0], lookup_table.shape[0]), 1)
    return jnp.sum(jnp.where(queries[:, None] == columns, lookup_table[None, :], 0), axis=1)


def remote(src, dst, send_sem, recv_sem, device_id):
    copy = pltpu.make_async_remote_copy(
        src_ref=src, dst_ref=dst, send_sem=send_sem, recv_sem=recv_sem,
        device_id=device_id, device_id_type=MESH,
    )
    copy.start()
    return copy


def send_strips(amp_ref, strips, send_sem, recv_sem, m, coup_total):
    rows = strips.shape[2]
    copies = []
    for d in range(1, coup_total):
        q = lax.rem(m + d, coup_total)
        copies.append(remote(
            amp_ref.at[:, pl.ds(pl.multiple_of(q * rows, 16), rows), :],
            strips.at[m], send_sem.at[d], recv_sem.at[d], {"coup": q},
        ))
    strips[m] = amp_ref[:, pl.ds(pl.multiple_of(m * rows, 16), rows), :]
    return copies


def send_picks(wanted, strips, outbuf, arrived, send_sem, recv_sem, g, group_total):
    pair_dev = strips.shape[1]
    copies = []
    for d in list(range(1, group_total)) + [0]:
        h = lax.rem(g + d, group_total)
        pick = wanted[h, 0, 0]
        if pair_dev == 1:
            block = strips[pick, 0]
        else:
            block = strips[pick // pair_dev, pick % pair_dev]
        if d == 0:
            arrived[g] = block
        else:
            outbuf[d] = block
            copies.append(remote(
                outbuf.at[d], arrived.at[g], send_sem.at[d], recv_sem.at[d], {"pairs": h}
            ))
    return copies


def greet(coords_list):
    barrier = pltpu.get_barrier_semaphore()
    for coords in coords_list:
        pl.semaphore_signal(barrier, inc=1, device_id=coords, device_id_type=MESH)
    pl.semaphore_wait(barrier, len(coords_list))


def first_exchange(
    group_total, coup_total, amp_ref, ask_ref, x_ref, arrived, x_all, asked, strips, outbuf, wanted,
    strip_send, strip_recv, ask_send, ask_recv, pick_send, pick_recv,
    far_send, far_recv, sib_send, sib_recv, fwd_send, fwd_recv, local_sem, want_sem,
):
    g, m = lax.axis_index("pairs"), lax.axis_index("coup")
    ov_dev = x_ref.shape[0]
    chips = coup_total // 2
    chip, core = m // 2, lax.rem(m, 2)
    sibling = chip * 2 + 1 - core
    greet(
        [{"coup": lax.rem(m + d, coup_total)} for d in range(1, coup_total)]
        + [{"pairs": lax.rem(g + d, group_total)} for d in range(1, group_total)]
    )
    strip_copies = send_strips(amp_ref, strips, strip_send, strip_recv, m, coup_total)
    ask_copies = []
    for d in range(1, group_total):
        h = lax.rem(g + d, group_total)
        ask_copies.append(remote(
            ask_ref.at[h], asked.at[g], ask_send.at[d], ask_recv.at[d], {"pairs": h}
        ))
    asked[g] = ask_ref[g]
    far_copies = []
    for i in range(ov_dev):
        for d in range(1, chips):
            peer = lax.rem(chip + d, chips) * 2 + core
            far_copies.append((d, i, remote(
                x_ref.at[i], x_all.at[m * ov_dev + i],
                far_send.at[d, i], far_recv.at[d, i], {"coup": peer},
            )))
    sib_copy = remote(
        x_ref, x_all.at[pl.ds(m * ov_dev, ov_dev)], sib_send, sib_recv, {"coup": sibling}
    )
    own_copy = pltpu.make_async_copy(x_ref, x_all.at[pl.ds(m * ov_dev, ov_dev)], local_sem)
    own_copy.start()
    for copy in ask_copies:
        copy.wait_recv()
    want_copy = pltpu.make_async_copy(asked, wanted, want_sem)
    want_copy.start()
    want_copy.wait()
    for copy in strip_copies:
        copy.wait_recv()
    pick_copies = send_picks(
        wanted, strips, outbuf, arrived, pick_send, pick_recv, g, group_total
    )
    forwards = []
    for d, i, copy in far_copies:
        copy.wait_recv()
        origin = lax.rem(chip - d + chips, chips) * 2 + core
        slot = x_all.at[origin * ov_dev + i]
        forwards.append(remote(
            slot, slot, fwd_send.at[d, i], fwd_recv.at[d, i], {"coup": sibling}
        ))
    own_copy.wait()
    sib_copy.wait()
    for copy in forwards + pick_copies:
        copy.wait()
    for copy in strip_copies + ask_copies + [c for _, _, c in far_copies]:
        copy.wait_send()


def later_exchange(
    group_total, coup_total, amp_ref, wanted, arrived, strips, outbuf,
    strip_send, strip_recv, pick_send, pick_recv,
):
    g, m = lax.axis_index("pairs"), lax.axis_index("coup")
    greet(
        [{"coup": lax.rem(m + d, coup_total)} for d in range(1, coup_total)]
        + [{"pairs": lax.rem(g + d, group_total)} for d in range(1, group_total)]
    )
    strip_copies = send_strips(amp_ref, strips, strip_send, strip_recv, m, coup_total)
    for copy in strip_copies:
        copy.wait_recv()
    pick_copies = send_picks(
        wanted, strips, outbuf, arrived, pick_send, pick_recv, g, group_total
    )
    for copy in pick_copies:
        copy.wait()
    for copy in strip_copies:
        copy.wait_send()


def reduce_partials(
    coup_total, chunks, part, total, near, joined, far, near_send, near_recv, far_send, far_recv
):
    m = lax.axis_index("coup")
    chips = coup_total // 2
    chip, core = m // 2, lax.rem(m, 2)
    sibling = chip * 2 + 1 - core
    peers = [lax.rem(chip + d, chips) * 2 for d in range(chips)]
    size = total.shape[1] // chunks
    rows = [slice(c * size, (c + 1) * size) for c in range(chunks)]
    order = [(d, c) for d in list(range(1, chips)) + [0] for c in range(chunks)]
    greet([{"coup": sibling}] + [{"coup": peers[d] + core} for d in range(1, chips)])
    near_copies = {}
    for d, c in order:
        near_copies[d, c] = remote(
            part.at[peers[d] + 1 - core, :, rows[c]], near.at[d, :, rows[c]],
            near_send.at[d, c], near_recv.at[d, c], {"coup": sibling},
        )
    far_copies = []
    for d, c in order:
        near_copies[d, c].wait_recv()
        both = part[peers[d] + core, :, rows[c]].astype(jnp.float32)
        both += near[d, :, rows[c]].astype(jnp.float32)
        if d == 0:
            total[:, rows[c]] = both
        else:
            joined[d, :, rows[c]] = both.astype(jnp.bfloat16)
            far_copies.append((d, c, remote(
                joined.at[d, :, rows[c]], far.at[d, :, rows[c]],
                far_send.at[d, c], far_recv.at[d, c], {"coup": peers[d] + core},
            )))
    for d, c, copy in far_copies:
        copy.wait_recv()
        total[:, rows[c]] += far[d, :, rows[c]].astype(jnp.float32)
    for _, _, copy in far_copies:
        copy.wait_send()
    for d, c in order:
        near_copies[d, c].wait_send()


def couple(coup_total, batch, x_index, source, owner, member, weight, amp_ref, *refs):
    x_refs, (out_ref, acc, padded) = refs[:batch], refs[batch:]
    k = pl.program_id(0)
    rows, width = amp_ref.shape[1:]

    @pl.when(k == 0)
    def _():
        acc[...] = jnp.zeros_like(acc)
        padded[...] = jnp.zeros_like(padded)

    def step(low):
        first = low // 128 * 128
        last = min(pl.cdiv(low + rows, 128) * 128, width)
        for b in range(batch):
            right = lax.dot_general(
                amp_ref[source[k * batch + b]], x_refs[b][0],
                (((1,), (1,)), ((), ())), preferred_element_type=jnp.float32,
            )
            padded[b, low:low + rows] = (right * weight[k * batch + b]).astype(jnp.bfloat16)
        for b in range(batch):
            acc[owner[k * batch + b]] += jnp.dot(
                x_refs[b][0, :, first:last], padded[b, first:last],
                preferred_element_type=jnp.float32,
            )

    for q in range(coup_total):
        pl.when(member[0] == q)(functools.partial(step, q * rows))

    @pl.when(k == pl.num_programs(0) - 1)
    def _():
        for p in range(acc.shape[0]):
            out_ref[p] = acc[p].astype(jnp.bfloat16)


def per_device(
    coupling_list, pair_slot, coupling_weight, integrals, orbital_energy, pair_energy, intersections
):
    group_total = lax.axis_size("pairs")
    coup_total = lax.axis_size("coup")
    group_index = lax.axis_index("pairs")
    member = lax.axis_index("coup")
    pair_dev, width = integrals.shape[0], integrals.shape[-1]
    ov_dev = intersections.shape[0]
    group_pairs = pair_dev * coup_total
    couplings = coupling_list.shape[1]
    rows = width // coup_total
    chips = coup_total // 2
    batch = math.gcd(couplings, 4)
    chunks = math.gcd(width // 16, 4)

    owner_row = lookup(pair_slot, coupling_list[0])
    reader_row = lookup(pair_slot, coupling_list[1])
    owner = owner_row - group_index * group_pairs
    source = reader_row // group_pairs
    x_index = coupling_list[2] - group_index * (ov_dev * coup_total)
    sources = lax.broadcasted_iota(jnp.int32, (group_total, couplings), 0)
    ask = jnp.max(
        jnp.where(source[None, :] == sources, (reader_row % group_pairs)[None, :], 0), axis=1
    )
    ask = jnp.broadcast_to(ask[:, None, None], (group_total, 8, 128))

    denominator = (
        orbital_energy[:, :, None] + orbital_energy[:, None, :] + pair_energy[:, None, None]
    )
    integral_f = integrals.astype(jnp.float32)
    rounded = (-integral_f / denominator).astype(jnp.bfloat16)

    vmem = pl.BlockSpec(memory_space=pltpu.VMEM)
    smem = pl.BlockSpec(memory_space=pltpu.SMEM)
    anywhere = pl.BlockSpec(memory_space=pl.ANY)
    dma = pltpu.SemaphoreType.DMA
    arrived_shape = jax.ShapeDtypeStruct((group_total, rows, width), jnp.bfloat16)
    strips_scratch = pltpu.VMEM((coup_total, pair_dev, rows, width), jnp.bfloat16)
    out_scratch = pltpu.VMEM((group_total, rows, width), jnp.bfloat16)

    def params(collective_id):
        return pltpu.CompilerParams(
            collective_id=collective_id, has_side_effects=True, vmem_limit_bytes=VMEM_LIMIT
        )

    arrived, x_all, asked = pl.pallas_call(
        functools.partial(first_exchange, group_total, coup_total),
        out_shape=(
            arrived_shape,
            jax.ShapeDtypeStruct((ov_dev * coup_total, width, width), jnp.bfloat16),
            jax.ShapeDtypeStruct((group_total, 8, 128), jnp.int32),
        ),
        in_specs=[vmem, vmem, anywhere],
        out_specs=(vmem, anywhere, vmem),
        scratch_shapes=[
            strips_scratch, out_scratch, pltpu.SMEM((group_total, 8, 128), jnp.int32),
            dma((coup_total,)), dma((coup_total,)), dma((group_total,)), dma((group_total,)),
            dma((group_total,)), dma((group_total,)),
            dma((chips, ov_dev)), dma((chips, ov_dev)), dma, dma,
            dma((chips, ov_dev)), dma((chips, ov_dev)), dma, dma,
        ],
        compiler_params=params(0),
        name="first_exchange",
    )(rounded, ask, intersections)

    for iteration in range(ITERS):
        if iteration > 0:
            arrived = pl.pallas_call(
                functools.partial(later_exchange, group_total, coup_total),
                out_shape=arrived_shape,
                in_specs=[vmem, smem],
                out_specs=vmem,
                scratch_shapes=[
                    strips_scratch, out_scratch,
                    dma((coup_total,)), dma((coup_total,)), dma((group_total,)), dma((group_total,)),
                ],
                compiler_params=params(1),
                name="later_exchange",
            )(rounded, asked)
        part = pl.pallas_call(
            functools.partial(couple, coup_total, batch),
            out_shape=jax.ShapeDtypeStruct((group_pairs, width, width), jnp.bfloat16),
            grid_spec=pltpu.PrefetchScalarGridSpec(
                num_scalar_prefetch=4,
                grid=(couplings // batch,),
                in_specs=[
                    smem,
                    pl.BlockSpec((group_total, rows, width), lambda k, *_: (0, 0, 0)),
                ] + [
                    pl.BlockSpec((1, width, width), lambda k, xi, *_, b=b: (xi[k * batch + b], 0, 0))
                    for b in range(batch)
                ],
                out_specs=pl.BlockSpec((group_pairs, width, width), lambda k, *_: (0, 0, 0)),
                scratch_shapes=[
                    pltpu.VMEM((group_pairs, width, width), jnp.float32),
                    pltpu.VMEM((batch, width, width), jnp.bfloat16),
                ],
            ),
            compiler_params=pltpu.CompilerParams(vmem_limit_bytes=VMEM_LIMIT),
            name="couple",
        )(x_index, source, owner, member[None], coupling_weight, arrived, *[x_all] * batch)
        block = (pair_dev, width, width)
        coupled = pl.pallas_call(
            functools.partial(reduce_partials, coup_total, chunks),
            out_shape=jax.ShapeDtypeStruct(block, jnp.float32),
            in_specs=[vmem],
            out_specs=vmem,
            scratch_shapes=[
                pltpu.VMEM((chips,) + block, jnp.bfloat16),
                pltpu.VMEM((chips,) + block, jnp.bfloat16),
                pltpu.VMEM((chips,) + block, jnp.bfloat16),
                *[dma((chips, chunks))] * 4,
            ],
            compiler_params=params(2),
            name="reduce_partials",
        )(part.reshape((coup_total,) + block))
        amplitudes = -(integral_f + coupled) / denominator
        rounded = amplitudes.astype(jnp.bfloat16)
    return amplitudes


def solution(mesh):
    in_specs = (
        P(None, "pairs"),
        P(),
        P("pairs"),
        P(("pairs", "coup"), None, None),
        P(("pairs", "coup"), None),
        P(("pairs", "coup")),
        P(("pairs", "coup"), None, None),
    )
    out_specs = P(("pairs", "coup"), None, None)
    return jax.shard_map(
        per_device, mesh=mesh, in_specs=in_specs, out_specs=out_specs, check_vma=False
    )
```

```python
import functools
import math

import jax
import jax.numpy as jnp
from jax import lax
from jax.experimental import pallas as pl
from jax.experimental.pallas import tpu as pltpu
from jax.sharding import PartitionSpec as P

ITERS = 2
MESH = pl.DeviceIdType.MESH
VMEM_LIMIT = 48 * 1024 * 1024


def lookup(lookup_table, queries):
    columns = lax.broadcasted_iota(jnp.int32, (queries.shape[0], lookup_table.shape[0]), 1)
    return jnp.sum(jnp.where(queries[:, None] == columns, lookup_table[None, :], 0), axis=1)


def remote(src, dst, send_sem, recv_sem, device_id):
    copy = pltpu.make_async_remote_copy(
        src_ref=src, dst_ref=dst, send_sem=send_sem, recv_sem=recv_sem,
        device_id=device_id, device_id_type=MESH,
    )
    copy.start()
    return copy


def send_strips(amp_ref, strips, send_sem, recv_sem, m, coup_total):
    rows = strips.shape[2]
    copies = []
    for d in range(1, coup_total):
        q = lax.rem(m + d, coup_total)
        copies.append(remote(
            amp_ref.at[:, pl.ds(pl.multiple_of(q * rows, 16), rows), :],
            strips.at[m], send_sem.at[d], recv_sem.at[d], {"coup": q},
        ))
    strips[m] = amp_ref[:, pl.ds(pl.multiple_of(m * rows, 16), rows), :]
    return copies


def send_picks(wanted, strips, outbuf, arrived, send_sem, recv_sem, g, group_total):
    pair_dev = strips.shape[1]
    copies = []
    for d in list(range(1, group_total)) + [0]:
        h = lax.rem(g + d, group_total)
        pick = wanted[h, 0, 0]
        if pair_dev == 1:
            block = strips[pick, 0]
        else:
            block = strips[pick // pair_dev, pick % pair_dev]
        if d == 0:
            arrived[g] = block
        else:
            outbuf[d] = block
            copies.append(remote(
                outbuf.at[d], arrived.at[g], send_sem.at[d], recv_sem.at[d], {"pairs": h}
            ))
    return copies


def greet(coords_list):
    barrier = pltpu.get_barrier_semaphore()
    for coords in coords_list:
        pl.semaphore_signal(barrier, inc=1, device_id=coords, device_id_type=MESH)
    pl.semaphore_wait(barrier, len(coords_list))


def first_exchange(
    group_total, coup_total, amp_ref, ask_ref, x_ref, tail_ref, arrived, x_all, asked, strips, outbuf, wanted,
    packed, packed_in, unpacked,
    strip_send, strip_recv, ask_send, ask_recv, pick_send, pick_recv,
    far_send, far_recv, sib_send, sib_recv, fwd_send, fwd_recv, local_sem, want_sem, put_sem,
):
    g, m = lax.axis_index("pairs"), lax.axis_index("coup")
    ov_dev = x_ref.shape[0]
    chips = coup_total // 2
    chip, core = m // 2, lax.rem(m, 2)
    sibling = chip * 2 + 1 - core
    greet(
        [{"coup": lax.rem(m + d, coup_total)} for d in range(1, coup_total)]
        + [{"pairs": lax.rem(g + d, group_total)} for d in range(1, group_total)]
    )
    strip_copies = send_strips(amp_ref, strips, strip_send, strip_recv, m, coup_total)
    ask_copies = []
    for d in range(1, group_total):
        h = lax.rem(g + d, group_total)
        ask_copies.append(remote(
            ask_ref.at[h], asked.at[g], ask_send.at[d], ask_recv.at[d], {"pairs": h}
        ))
    asked[g] = ask_ref[g]
    half = x_ref.shape[1] // 2
    main = x_all.shape[2] - tail_ref.shape[2]
    narrow = x_ref.shape[2] - main
    low, high = pl.ds(0, main), pl.ds(main, tail_ref.shape[2])
    mine = pl.ds(m * ov_dev, ov_dev)
    far_copies = []
    for i in range(ov_dev):
        packed[i] = jnp.concatenate(
            [tail_ref[i, :half, :narrow], tail_ref[i, half:, :narrow]], axis=-1
        )
        for d in range(1, chips):
            peer = {"coup": lax.rem(chip + d, chips) * 2 + core}
            far_copies.append((d, i, remote(
                x_ref.at[i, :, low], x_all.at[m * ov_dev + i, :, low],
                far_send.at[0, d, i], far_recv.at[0, d, i], peer,
            ), remote(
                packed.at[i], packed_in.at[d, i],
                far_send.at[1, d, i], far_recv.at[1, d, i], peer,
            )))
    near_copies = [
        remote(x_ref.at[:, :, low], x_all.at[mine, :, low],
               sib_send.at[0], sib_recv.at[0], {"coup": sibling}),
        remote(tail_ref, x_all.at[mine, :, high],
               sib_send.at[1], sib_recv.at[1], {"coup": sibling}),
    ]
    own_copies = [
        pltpu.make_async_copy(x_ref.at[:, :, low], x_all.at[mine, :, low], local_sem.at[0]),
        pltpu.make_async_copy(tail_ref, x_all.at[mine, :, high], local_sem.at[1]),
    ]
    for copy in own_copies:
        copy.start()
    for copy in ask_copies:
        copy.wait_recv()
    want_copy = pltpu.make_async_copy(asked, wanted, want_sem)
    want_copy.start()
    want_copy.wait()
    for copy in strip_copies:
        copy.wait_recv()
    pick_copies = send_picks(
        wanted, strips, outbuf, arrived, pick_send, pick_recv, g, group_total
    )
    forwards = []
    for d, i, main_copy, tail_copy in far_copies:
        origin = lax.rem(chip - d + chips, chips) * 2 + core
        slot = origin * ov_dev + i
        main_copy.wait_recv()
        there = x_all.at[slot, :, low]
        forwards.append(remote(
            there, there, fwd_send.at[0, d, i], fwd_recv.at[0, d, i], {"coup": sibling}
        ))
        tail_copy.wait_recv()
        block = packed_in[d, i]
        unpacked[d, i, :half] = block
        unpacked[d, i, half:] = jnp.concatenate([block[:, narrow:], block[:, :narrow]], axis=-1)
        there = x_all.at[slot, :, high]
        forwards.append(remote(
            unpacked.at[d, i], there, fwd_send.at[1, d, i], fwd_recv.at[1, d, i],
            {"coup": sibling},
        ))
        put = pltpu.make_async_copy(unpacked.at[d, i], there, put_sem.at[d, i])
        put.start()
        own_copies.append(put)
    for copy in own_copies + near_copies + forwards + pick_copies:
        copy.wait()
    for copy in strip_copies + ask_copies + [c for far in far_copies for c in far[2:]]:
        copy.wait_send()


def later_exchange(
    group_total, coup_total, amp_ref, wanted, arrived, strips, outbuf,
    strip_send, strip_recv, pick_send, pick_recv,
):
    g, m = lax.axis_index("pairs"), lax.axis_index("coup")
    greet(
        [{"coup": lax.rem(m + d, coup_total)} for d in range(1, coup_total)]
        + [{"pairs": lax.rem(g + d, group_total)} for d in range(1, group_total)]
    )
    strip_copies = send_strips(amp_ref, strips, strip_send, strip_recv, m, coup_total)
    for copy in strip_copies:
        copy.wait_recv()
    pick_copies = send_picks(
        wanted, strips, outbuf, arrived, pick_send, pick_recv, g, group_total
    )
    for copy in pick_copies:
        copy.wait()
    for copy in strip_copies:
        copy.wait_send()


def reduce_partials(
    coup_total, chunks, part, total, near, joined, far, near_send, near_recv, far_send, far_recv
):
    m = lax.axis_index("coup")
    chips = coup_total // 2
    chip, core = m // 2, lax.rem(m, 2)
    sibling = chip * 2 + 1 - core
    peers = [lax.rem(chip + d, chips) * 2 for d in range(chips)]
    size = total.shape[1] // chunks
    rows = [slice(c * size, (c + 1) * size) for c in range(chunks)]
    order = [(d, c) for d in list(range(1, chips)) + [0] for c in range(chunks)]
    greet([{"coup": sibling}] + [{"coup": peers[d] + core} for d in range(1, chips)])
    near_copies = {}
    for d, c in order:
        near_copies[d, c] = remote(
            part.at[peers[d] + 1 - core, :, rows[c]], near.at[d, :, rows[c]],
            near_send.at[d, c], near_recv.at[d, c], {"coup": sibling},
        )
    far_copies = []
    for d, c in order:
        near_copies[d, c].wait_recv()
        both = part[peers[d] + core, :, rows[c]].astype(jnp.float32)
        both += near[d, :, rows[c]].astype(jnp.float32)
        if d == 0:
            total[:, rows[c]] = both
        else:
            joined[d, :, rows[c]] = both.astype(jnp.bfloat16)
            far_copies.append((d, c, remote(
                joined.at[d, :, rows[c]], far.at[d, :, rows[c]],
                far_send.at[d, c], far_recv.at[d, c], {"coup": peers[d] + core},
            )))
    for d, c, copy in far_copies:
        copy.wait_recv()
        total[:, rows[c]] += far[d, :, rows[c]].astype(jnp.float32)
    for _, _, copy in far_copies:
        copy.wait_send()
    for d, c in order:
        near_copies[d, c].wait_send()


def couple(coup_total, batch, x_index, source, owner, member, weight, amp_ref, *refs):
    x_refs, (out_ref, acc, padded) = refs[:batch], refs[batch:]
    k = pl.program_id(0)
    rows, width = amp_ref.shape[1:]

    @pl.when(k == 0)
    def _():
        acc[...] = jnp.zeros_like(acc)
        padded[...] = jnp.zeros_like(padded)

    def step(low):
        first = low // 128 * 128
        last = min(pl.cdiv(low + rows, 128) * 128, width)
        for b in range(batch):
            right = lax.dot_general(
                amp_ref[source[k * batch + b]], x_refs[b][0, :, :width],
                (((1,), (1,)), ((), ())), preferred_element_type=jnp.float32,
            )
            padded[b, low:low + rows] = (right * weight[k * batch + b]).astype(jnp.bfloat16)
        for b in range(batch):
            acc[owner[k * batch + b]] += jnp.dot(
                x_refs[b][0, :, first:last], padded[b, first:last],
                preferred_element_type=jnp.float32,
            )

    for q in range(coup_total):
        pl.when(member[0] == q)(functools.partial(step, q * rows))

    @pl.when(k == pl.num_programs(0) - 1)
    def _():
        for p in range(acc.shape[0]):
            out_ref[p] = acc[p].astype(jnp.bfloat16)


def per_device(
    coupling_list, pair_slot, coupling_weight, integrals, orbital_energy, pair_energy, intersections
):
    group_total = lax.axis_size("pairs")
    coup_total = lax.axis_size("coup")
    group_index = lax.axis_index("pairs")
    member = lax.axis_index("coup")
    pair_dev, width = integrals.shape[0], integrals.shape[-1]
    ov_dev = intersections.shape[0]
    group_pairs = pair_dev * coup_total
    couplings = coupling_list.shape[1]
    rows = width // coup_total
    chips = coup_total // 2
    batch = math.gcd(couplings, 4)
    chunks = math.gcd(width // 16, 4)

    owner_row = lookup(pair_slot, coupling_list[0])
    reader_row = lookup(pair_slot, coupling_list[1])
    owner = owner_row - group_index * group_pairs
    source = reader_row // group_pairs
    x_index = coupling_list[2] - group_index * (ov_dev * coup_total)
    sources = lax.broadcasted_iota(jnp.int32, (group_total, couplings), 0)
    ask = jnp.max(
        jnp.where(source[None, :] == sources, (reader_row % group_pairs)[None, :], 0), axis=1
    )
    ask = jnp.broadcast_to(ask[:, None, None], (group_total, 8, 128))

    denominator = (
        orbital_energy[:, :, None] + orbital_energy[:, None, :] + pair_energy[:, None, None]
    )
    integral_f = integrals.astype(jnp.float32)
    rounded = (-integral_f / denominator).astype(jnp.bfloat16)

    wide = pl.cdiv(width, 128) * 128
    tails = jnp.pad(intersections[:, :, wide - 128:], ((0, 0), (0, 0), (0, wide - width)))

    vmem = pl.BlockSpec(memory_space=pltpu.VMEM)
    smem = pl.BlockSpec(memory_space=pltpu.SMEM)
    anywhere = pl.BlockSpec(memory_space=pl.ANY)
    dma = pltpu.SemaphoreType.DMA
    arrived_shape = jax.ShapeDtypeStruct((group_total, rows, width), jnp.bfloat16)
    strips_scratch = pltpu.VMEM((coup_total, pair_dev, rows, width), jnp.bfloat16)
    out_scratch = pltpu.VMEM((group_total, rows, width), jnp.bfloat16)

    def params(collective_id):
        return pltpu.CompilerParams(
            collective_id=collective_id, has_side_effects=True, vmem_limit_bytes=VMEM_LIMIT
        )

    arrived, x_all, asked = pl.pallas_call(
        functools.partial(first_exchange, group_total, coup_total),
        out_shape=(
            arrived_shape,
            jax.ShapeDtypeStruct((ov_dev * coup_total, width, wide), jnp.bfloat16),
            jax.ShapeDtypeStruct((group_total, 8, 128), jnp.int32),
        ),
        in_specs=[vmem, vmem, anywhere, vmem],
        out_specs=(vmem, anywhere, vmem),
        scratch_shapes=[
            strips_scratch, out_scratch, pltpu.SMEM((group_total, 8, 128), jnp.int32),
            pltpu.VMEM((ov_dev, width // 2, 128), jnp.bfloat16),
            pltpu.VMEM((chips, ov_dev, width // 2, 128), jnp.bfloat16),
            pltpu.VMEM((chips, ov_dev, width, 128), jnp.bfloat16),
            dma((coup_total,)), dma((coup_total,)), dma((group_total,)), dma((group_total,)),
            dma((group_total,)), dma((group_total,)),
            dma((2, chips, ov_dev)), dma((2, chips, ov_dev)), dma((2,)), dma((2,)),
            dma((2, chips, ov_dev)), dma((2, chips, ov_dev)), dma((2,)), dma,
            dma((chips, ov_dev)),
        ],
        compiler_params=params(0),
        name="first_exchange",
    )(rounded, ask, intersections, tails)

    for iteration in range(ITERS):
        if iteration > 0:
            arrived = pl.pallas_call(
                functools.partial(later_exchange, group_total, coup_total),
                out_shape=arrived_shape,
                in_specs=[vmem, smem],
                out_specs=vmem,
                scratch_shapes=[
                    strips_scratch, out_scratch,
                    dma((coup_total,)), dma((coup_total,)), dma((group_total,)), dma((group_total,)),
                ],
                compiler_params=params(1),
                name="later_exchange",
            )(rounded, asked)
        part = pl.pallas_call(
            functools.partial(couple, coup_total, batch),
            out_shape=jax.ShapeDtypeStruct((group_pairs, width, width), jnp.bfloat16),
            grid_spec=pltpu.PrefetchScalarGridSpec(
                num_scalar_prefetch=4,
                grid=(couplings // batch,),
                in_specs=[
                    smem,
                    pl.BlockSpec((group_total, rows, width), lambda k, *_: (0, 0, 0)),
                ] + [
                    pl.BlockSpec((1, width, wide), lambda k, xi, *_, b=b: (xi[k * batch + b], 0, 0))
                    for b in range(batch)
                ],
                out_specs=pl.BlockSpec((group_pairs, width, width), lambda k, *_: (0, 0, 0)),
                scratch_shapes=[
                    pltpu.VMEM((group_pairs, width, width), jnp.float32),
                    pltpu.VMEM((batch, width, width), jnp.bfloat16),
                ],
            ),
            compiler_params=pltpu.CompilerParams(vmem_limit_bytes=VMEM_LIMIT),
            name="couple",
        )(x_index, source, owner, member[None], coupling_weight, arrived, *[x_all] * batch)
        block = (pair_dev, width, width)
        coupled = pl.pallas_call(
            functools.partial(reduce_partials, coup_total, chunks),
            out_shape=jax.ShapeDtypeStruct(block, jnp.float32),
            in_specs=[vmem],
            out_specs=vmem,
            scratch_shapes=[
                pltpu.VMEM((chips,) + block, jnp.bfloat16),
                pltpu.VMEM((chips,) + block, jnp.bfloat16),
                pltpu.VMEM((chips,) + block, jnp.bfloat16),
                *[dma((chips, chunks))] * 4,
            ],
            compiler_params=params(2),
            name="reduce_partials",
        )(part.reshape((coup_total,) + block))
        amplitudes = -(integral_f + coupled) / denominator
        rounded = amplitudes.astype(jnp.bfloat16)
    return amplitudes


def solution(mesh):
    in_specs = (
        P(None, "pairs"),
        P(),
        P("pairs"),
        P(("pairs", "coup"), None, None),
        P(("pairs", "coup"), None),
        P(("pairs", "coup")),
        P(("pairs", "coup"), None, None),
    )
    out_specs = P(("pairs", "coup"), None, None)
    return jax.shard_map(
        per_device, mesh=mesh, in_specs=in_specs, out_specs=out_specs, check_vma=False
    )
```

```python
import functools
import math

import jax
import jax.numpy as jnp
from jax import lax
from jax.experimental import pallas as pl
from jax.experimental.pallas import tpu as pltpu
from jax.sharding import PartitionSpec as P

ITERS = 2
MESH = pl.DeviceIdType.MESH
VMEM_LIMIT = 48 * 1024 * 1024


def lookup(lookup_table, queries):
    columns = lax.broadcasted_iota(jnp.int32, (queries.shape[0], lookup_table.shape[0]), 1)
    return jnp.sum(jnp.where(queries[:, None] == columns, lookup_table[None, :], 0), axis=1)


def remote(src, dst, send_sem, recv_sem, device_id):
    copy = pltpu.make_async_remote_copy(
        src_ref=src, dst_ref=dst, send_sem=send_sem, recv_sem=recv_sem,
        device_id=device_id, device_id_type=MESH,
    )
    copy.start()
    return copy


def send_strips(amp_ref, strips, send_sem, recv_sem, m, coup_total):
    rows = strips.shape[2]
    copies = []
    for d in range(1, coup_total):
        q = lax.rem(m + d, coup_total)
        copies.append(remote(
            amp_ref.at[:, pl.ds(pl.multiple_of(q * rows, 16), rows), :],
            strips.at[m], send_sem.at[d], recv_sem.at[d], {"coup": q},
        ))
    strips[m] = amp_ref[:, pl.ds(pl.multiple_of(m * rows, 16), rows), :]
    return copies


def send_picks(wanted, strips, outbuf, arrived, send_sem, recv_sem, g, group_total):
    pair_dev = strips.shape[1]
    copies = []
    for d in list(range(1, group_total)) + [0]:
        h = lax.rem(g + d, group_total)
        pick = wanted[h, 0, 0]
        if pair_dev == 1:
            block = strips[pick, 0]
        else:
            block = strips[pick // pair_dev, pick % pair_dev]
        if d == 0:
            arrived[g] = block
        else:
            outbuf[d] = block
            copies.append(remote(
                outbuf.at[d], arrived.at[g], send_sem.at[d], recv_sem.at[d], {"pairs": h}
            ))
    return copies


def greet(coords_list):
    barrier = pltpu.get_barrier_semaphore()
    for coords in coords_list:
        pl.semaphore_signal(barrier, inc=1, device_id=coords, device_id_type=MESH)
    pl.semaphore_wait(barrier, len(coords_list))


def first_exchange(
    group_total, coup_total, amp_ref, ask_ref, x_ref, tail_ref, arrived, x_all, asked, strips, outbuf, wanted,
    packed, packed_in, unpacked,
    strip_send, strip_recv, ask_send, ask_recv, pick_send, pick_recv,
    far_send, far_recv, sib_send, sib_recv, fwd_send, fwd_recv, local_sem, want_sem, put_sem,
):
    g, m = lax.axis_index("pairs"), lax.axis_index("coup")
    ov_dev = x_ref.shape[0]
    chips = coup_total // 2
    chip, core = m // 2, lax.rem(m, 2)
    sibling = chip * 2 + 1 - core
    greet(
        [{"coup": lax.rem(m + d, coup_total)} for d in range(1, coup_total)]
        + [{"pairs": lax.rem(g + d, group_total)} for d in range(1, group_total)]
    )
    strip_copies = send_strips(amp_ref, strips, strip_send, strip_recv, m, coup_total)
    ask_copies = []
    for d in range(1, group_total):
        h = lax.rem(g + d, group_total)
        ask_copies.append(remote(
            ask_ref.at[h], asked.at[g], ask_send.at[d], ask_recv.at[d], {"pairs": h}
        ))
    asked[g] = ask_ref[g]
    half = x_ref.shape[1] // 2
    main = x_all.shape[2] - tail_ref.shape[2]
    narrow = x_ref.shape[2] - main
    low, high = pl.ds(0, main), pl.ds(main, tail_ref.shape[2])
    mine = pl.ds(m * ov_dev, ov_dev)
    far_copies = []
    for i in range(ov_dev):
        packed[i] = jnp.concatenate(
            [tail_ref[i, :half, :narrow], tail_ref[i, half:, :narrow]], axis=-1
        )
        for d in range(1, chips):
            peer = {"coup": lax.rem(chip + d, chips) * 2 + core}
            far_copies.append((d, i, remote(
                x_ref.at[i, :, low], x_all.at[m * ov_dev + i, :, low],
                far_send.at[0, d, i], far_recv.at[0, d, i], peer,
            ), remote(
                packed.at[i], packed_in.at[d, i],
                far_send.at[1, d, i], far_recv.at[1, d, i], peer,
            )))
    near_copies = [
        remote(x_ref.at[:, :, low], x_all.at[mine, :, low],
               sib_send.at[0], sib_recv.at[0], {"coup": sibling}),
        remote(tail_ref, x_all.at[mine, :, high],
               sib_send.at[1], sib_recv.at[1], {"coup": sibling}),
    ]
    own_copies = [
        pltpu.make_async_copy(x_ref.at[:, :, low], x_all.at[mine, :, low], local_sem.at[0]),
        pltpu.make_async_copy(tail_ref, x_all.at[mine, :, high], local_sem.at[1]),
    ]
    for copy in own_copies:
        copy.start()
    for copy in ask_copies:
        copy.wait_recv()
    want_copy = pltpu.make_async_copy(asked, wanted, want_sem)
    want_copy.start()
    want_copy.wait()
    for copy in strip_copies:
        copy.wait_recv()
    pick_copies = send_picks(
        wanted, strips, outbuf, arrived, pick_send, pick_recv, g, group_total
    )
    forwards = []
    for d, i, main_copy, tail_copy in far_copies:
        origin = lax.rem(chip - d + chips, chips) * 2 + core
        slot = origin * ov_dev + i
        main_copy.wait_recv()
        there = x_all.at[slot, :, low]
        forwards.append(remote(
            there, there, fwd_send.at[0, d, i], fwd_recv.at[0, d, i], {"coup": sibling}
        ))
        tail_copy.wait_recv()
        block = packed_in[d, i]
        unpacked[d, i, :half] = block
        unpacked[d, i, half:] = jnp.concatenate([block[:, narrow:], block[:, :narrow]], axis=-1)
        there = x_all.at[slot, :, high]
        forwards.append(remote(
            unpacked.at[d, i], there, fwd_send.at[1, d, i], fwd_recv.at[1, d, i],
            {"coup": sibling},
        ))
        put = pltpu.make_async_copy(unpacked.at[d, i], there, put_sem.at[d, i])
        put.start()
        own_copies.append(put)
    for copy in own_copies + near_copies + forwards + pick_copies:
        copy.wait()
    for copy in strip_copies + ask_copies + [c for far in far_copies for c in far[2:]]:
        copy.wait_send()


def later_exchange(
    group_total, coup_total, amp_ref, wanted, arrived, strips, outbuf,
    strip_send, strip_recv, pick_send, pick_recv,
):
    g, m = lax.axis_index("pairs"), lax.axis_index("coup")
    greet(
        [{"coup": lax.rem(m + d, coup_total)} for d in range(1, coup_total)]
        + [{"pairs": lax.rem(g + d, group_total)} for d in range(1, group_total)]
    )
    strip_copies = send_strips(amp_ref, strips, strip_send, strip_recv, m, coup_total)
    for copy in strip_copies:
        copy.wait_recv()
    pick_copies = send_picks(
        wanted, strips, outbuf, arrived, pick_send, pick_recv, g, group_total
    )
    for copy in pick_copies:
        copy.wait()
    for copy in strip_copies:
        copy.wait_send()


def reduce_partials(
    coup_total, chunks, part, total, near, joined, far, near_send, near_recv, far_send, far_recv
):
    m = lax.axis_index("coup")
    chips = coup_total // 2
    chip, core = m // 2, lax.rem(m, 2)
    sibling = chip * 2 + 1 - core
    peers = [lax.rem(chip + d, chips) * 2 for d in range(chips)]
    size = part.shape[2] // chunks
    rows = [slice(c * size, (c + 1) * size) for c in range(chunks)]
    order = [(d, c) for d in list(range(1, chips)) + [0] for c in range(chunks)]
    greet([{"coup": sibling}] + [{"coup": peers[d] + core} for d in range(1, chips)])
    near_copies = {}
    for d, c in order:
        near_copies[d, c] = remote(
            part.at[peers[d] + 1 - core, :, rows[c]], near.at[d, :, rows[c]],
            near_send.at[d, c], near_recv.at[d, c], {"coup": sibling},
        )
    far_copies = []
    far_copies = {}

    def own_chip(d, c):
        near_copies[d, c].wait_recv()
        both = part[peers[d] + core, :, rows[c]].astype(jnp.float32)
        return both + near[d, :, rows[c]].astype(jnp.float32)

    for d, c in order:
        if d > 0:
            joined[d, :, rows[c]] = own_chip(d, c).astype(jnp.bfloat16)
            far_copies[d, c] = remote(
                joined.at[d, :, rows[c]], far.at[d, :, rows[c]],
                far_send.at[d, c], far_recv.at[d, c], {"coup": peers[d] + core},
            )
    narrow = total.shape[2] % 128
    for c in range(chunks):
        value = own_chip(0, c)
        for d in range(1, chips):
            far_copies[d, c].wait_recv()
            value += far[d, :, rows[c]].astype(jnp.float32)
        left = c // 2 * 128
        if c < chunks - 1:
            total[:, c % 2 * size:(c % 2 + 1) * size, left:left + 128] = value
        else:
            total[:, :size, left:] = value[:, :, :narrow]
            total[:, size:, left:] = value[:, :, narrow:]
    for copy in far_copies.values():
        copy.wait_send()
    for d, c in order:
        near_copies[d, c].wait_send()


def couple(coup_total, batch, x_index, source, owner, member, weight, amp_ref, *refs):
    x_refs, (out_ref, acc, padded) = refs[:batch], refs[batch:]
    k = pl.program_id(0)
    rows, width = amp_ref.shape[1:]

    @pl.when(k == 0)
    def _():
        acc[...] = jnp.zeros_like(acc)
        padded[...] = jnp.zeros_like(padded)

    def step(low):
        first = low // 128 * 128
        last = min(pl.cdiv(low + rows, 128) * 128, width)
        for b in range(batch):
            right = lax.dot_general(
                amp_ref[source[k * batch + b]], x_refs[b][0, :, :width],
                (((1,), (1,)), ((), ())), preferred_element_type=jnp.float32,
            )
            padded[b, low:low + rows] = (right * weight[k * batch + b]).astype(jnp.bfloat16)
        for b in range(batch):
            acc[owner[k * batch + b]] += jnp.dot(
                x_refs[b][0, :, first:last], padded[b, first:last],
                preferred_element_type=jnp.float32,
            )

    for q in range(coup_total):
        pl.when(member[0] == q)(functools.partial(step, q * rows))

    @pl.when(k == pl.num_programs(0) - 1)
    def _():
        for p in range(acc.shape[0]):
            for left in range(0, width - 127, 128):
                out_ref[p, left // 128 * width:(left // 128 + 1) * width] = (
                    acc[p, :, left:left + 128].astype(jnp.bfloat16)
                )
            left = width // 128 * 128
            out_ref[p, left // 128 * width:] = jnp.concatenate(
                [acc[p, :width // 2, left:], acc[p, width // 2:, left:]], axis=-1
            ).astype(jnp.bfloat16)


def per_device(
    coupling_list, pair_slot, coupling_weight, integrals, orbital_energy, pair_energy, intersections
):
    group_total = lax.axis_size("pairs")
    coup_total = lax.axis_size("coup")
    group_index = lax.axis_index("pairs")
    member = lax.axis_index("coup")
    pair_dev, width = integrals.shape[0], integrals.shape[-1]
    ov_dev = intersections.shape[0]
    group_pairs = pair_dev * coup_total
    couplings = coupling_list.shape[1]
    rows = width // coup_total
    chips = coup_total // 2
    batch = math.gcd(couplings, 4)
    chunks = width // 64
    stacked = chunks * (width // 2)

    owner_row = lookup(pair_slot, coupling_list[0])
    reader_row = lookup(pair_slot, coupling_list[1])
    owner = owner_row - group_index * group_pairs
    source = reader_row // group_pairs
    x_index = coupling_list[2] - group_index * (ov_dev * coup_total)
    sources = lax.broadcasted_iota(jnp.int32, (group_total, couplings), 0)
    ask = jnp.max(
        jnp.where(source[None, :] == sources, (reader_row % group_pairs)[None, :], 0), axis=1
    )
    ask = jnp.broadcast_to(ask[:, None, None], (group_total, 8, 128))

    denominator = (
        orbital_energy[:, :, None] + orbital_energy[:, None, :] + pair_energy[:, None, None]
    )
    integral_f = integrals.astype(jnp.float32)
    rounded = (-integral_f / denominator).astype(jnp.bfloat16)

    wide = pl.cdiv(width, 128) * 128
    tails = jnp.pad(intersections[:, :, wide - 128:], ((0, 0), (0, 0), (0, wide - width)))

    vmem = pl.BlockSpec(memory_space=pltpu.VMEM)
    smem = pl.BlockSpec(memory_space=pltpu.SMEM)
    anywhere = pl.BlockSpec(memory_space=pl.ANY)
    dma = pltpu.SemaphoreType.DMA
    arrived_shape = jax.ShapeDtypeStruct((group_total, rows, width), jnp.bfloat16)
    strips_scratch = pltpu.VMEM((coup_total, pair_dev, rows, width), jnp.bfloat16)
    out_scratch = pltpu.VMEM((group_total, rows, width), jnp.bfloat16)

    def params(collective_id):
        return pltpu.CompilerParams(
            collective_id=collective_id, has_side_effects=True, vmem_limit_bytes=VMEM_LIMIT
        )

    arrived, x_all, asked = pl.pallas_call(
        functools.partial(first_exchange, group_total, coup_total),
        out_shape=(
            arrived_shape,
            jax.ShapeDtypeStruct((ov_dev * coup_total, width, wide), jnp.bfloat16),
            jax.ShapeDtypeStruct((group_total, 8, 128), jnp.int32),
        ),
        in_specs=[vmem, vmem, anywhere, vmem],
        out_specs=(vmem, anywhere, vmem),
        scratch_shapes=[
            strips_scratch, out_scratch, pltpu.SMEM((group_total, 8, 128), jnp.int32),
            pltpu.VMEM((ov_dev, width // 2, 128), jnp.bfloat16),
            pltpu.VMEM((chips, ov_dev, width // 2, 128), jnp.bfloat16),
            pltpu.VMEM((chips, ov_dev, width, 128), jnp.bfloat16),
            dma((coup_total,)), dma((coup_total,)), dma((group_total,)), dma((group_total,)),
            dma((group_total,)), dma((group_total,)),
            dma((2, chips, ov_dev)), dma((2, chips, ov_dev)), dma((2,)), dma((2,)),
            dma((2, chips, ov_dev)), dma((2, chips, ov_dev)), dma((2,)), dma,
            dma((chips, ov_dev)),
        ],
        compiler_params=params(0),
        name="first_exchange",
    )(rounded, ask, intersections, tails)

    for iteration in range(ITERS):
        if iteration > 0:
            arrived = pl.pallas_call(
                functools.partial(later_exchange, group_total, coup_total),
                out_shape=arrived_shape,
                in_specs=[vmem, smem],
                out_specs=vmem,
                scratch_shapes=[
                    strips_scratch, out_scratch,
                    dma((coup_total,)), dma((coup_total,)), dma((group_total,)), dma((group_total,)),
                ],
                compiler_params=params(1),
                name="later_exchange",
            )(rounded, asked)
        part = pl.pallas_call(
            functools.partial(couple, coup_total, batch),
            out_shape=jax.ShapeDtypeStruct((group_pairs, stacked, 128), jnp.bfloat16),
            grid_spec=pltpu.PrefetchScalarGridSpec(
                num_scalar_prefetch=4,
                grid=(couplings // batch,),
                in_specs=[
                    smem,
                    pl.BlockSpec((group_total, rows, width), lambda k, *_: (0, 0, 0)),
                ] + [
                    pl.BlockSpec((1, width, wide), lambda k, xi, *_, b=b: (xi[k * batch + b], 0, 0))
                    for b in range(batch)
                ],
                out_specs=pl.BlockSpec((group_pairs, stacked, 128), lambda k, *_: (0, 0, 0)),
                scratch_shapes=[
                    pltpu.VMEM((group_pairs, width, width), jnp.float32),
                    pltpu.VMEM((batch, width, width), jnp.bfloat16),
                ],
            ),
            compiler_params=pltpu.CompilerParams(vmem_limit_bytes=VMEM_LIMIT),
            name="couple",
        )(x_index, source, owner, member[None], coupling_weight, arrived, *[x_all] * batch)
        block = (pair_dev, width, width)
        packed_block = (pair_dev, stacked, 128)
        coupled = pl.pallas_call(
            functools.partial(reduce_partials, coup_total, chunks),
            out_shape=jax.ShapeDtypeStruct(block, jnp.float32),
            in_specs=[vmem],
            out_specs=vmem,
            scratch_shapes=[
                pltpu.VMEM((chips,) + packed_block, jnp.bfloat16),
                pltpu.VMEM((chips,) + packed_block, jnp.bfloat16),
                pltpu.VMEM((chips,) + packed_block, jnp.bfloat16),
                *[dma((chips, chunks))] * 4,
            ],
            compiler_params=params(2),
            name="reduce_partials",
        )(part.reshape((coup_total,) + packed_block))
        amplitudes = -(integral_f + coupled) / denominator
        rounded = amplitudes.astype(jnp.bfloat16)
    return amplitudes


def solution(mesh):
    in_specs = (
        P(None, "pairs"),
        P(),
        P("pairs"),
        P(("pairs", "coup"), None, None),
        P(("pairs", "coup"), None),
        P(("pairs", "coup")),
        P(("pairs", "coup"), None, None),
    )
    out_specs = P(("pairs", "coup"), None, None)
    return jax.shard_map(
        per_device, mesh=mesh, in_specs=in_specs, out_specs=out_specs, check_vma=False
    )
```
